32 devices in a mesh: row: 4 (over x, core), col: 8 (over z, y).
Axes of the slice: x: 2, y: 2, z: 4, core: 2. Of those that a mesh axis runs over, the one named last changes fastest.
Arguments:
- diag_coords: int32 [2, 1536], replicated, may hold values from 0 to 32767
- panel_coords: int32 [2, 8, 1536], P(None, 'row', 'col'), may hold values from 0 to 32767
- test_matrix: bfloat16 [8, 1536, 512], P('row', 'col'), may hold values from -6 to 6
- ranks: int32 [8], replicated, may hold values from 64 to 512, as said below
Outputs:
- panel_left: bfloat16 [8, 1536, 512], P('row', 'col')
- update_right: bfloat16 [8, 8, 1536, 512], P('row', 'col')
The draws below stay inside these ranges and needn't reach their ends.
Inputs may be any that keep to these rules, and one draw needn't show every extreme that they name: ranks[i] is 512 at tile 0 and 64 at the last tile and falls roughly evenly in between, with small random steps.
All inputs are finite; a program needn't handle non-finite values.
Results may differ from the reference program's by a relative error of at most 0.0068.
Values may be sent and summed in bfloat16 or wider, within the bound.
A program may use at most 256 MiB of HBM per device.

```python
import jax
import jax.numpy as jnp
from jax import lax

NB = 1536
R = 512
MT = 8


def draw_ranks(key, part):
    index = jnp.arange(MT, dtype=jnp.int32)
    base = R - (R - R // 8) * index // (MT - 1)
    jitter = jax.random.randint(key, (MT,), 0, R // 16 + 1)
    inner = ((index > 0) & (index < MT - 1)).astype(jnp.int32)
    values = jnp.maximum(base - jitter * inner, R // 8)
    return values.astype(jnp.int32)


def place_ends(entries, stream_key, least, top_value):
    extent = entries.shape
    place = [jax.random.randint(jax.random.fold_in(stream_key, axis), (), 0, extent[axis]) for axis in range(len(extent))]
    entries = entries.at[tuple(place)].set(least)
    longest = extent.index(max(extent))
    place[longest] = (place[longest] + 1) % extent[longest]
    return entries.at[tuple(place)].set(top_value)


def steps_of(own_key, shape, split, low, high):
    loudness, own = 1.0, jax.random.fold_in(own_key, 6)
    for axis_at, blocks in split:
        draws = jnp.exp(jax.random.uniform(jax.random.fold_in(own, axis_at), (blocks,), jnp.float32, low / len(split), high / len(split)))
        loudness = loudness * jnp.repeat(draws, shape[axis_at] // blocks).reshape([-1 if axis == axis_at else 1 for axis in range(len(shape))])
    return loudness


def noise(stream_key, extent, width, most, pieces=(), held_as=jnp.bfloat16):
    loudness = steps_of(stream_key, extent, pieces, -0.22, 0.18) if pieces else 1.0
    array = jax.random.normal(stream_key, extent, jnp.float32) * width * loudness
    return jnp.minimum(jnp.maximum(array, -most), most).astype(held_as)


def setup_inputs(seed: int = 0) -> dict:
    key_of = jax.random.split(jax.random.key(seed), 5)
    diag_coords = place_ends(jax.random.randint(key_of[0], (2, NB), 0, 32768), jax.random.fold_in(key_of[0], 1), 0, 32767).astype(jnp.int32)
    panel_coords = place_ends(jax.random.randint(key_of[1], (2, MT, NB), 0, 32768), jax.random.fold_in(key_of[1], 1), 0, 32767).astype(jnp.int32)
    test_matrix = noise(key_of[2], (MT, NB, R), 1.0, 6.0, ((0, 4), (1, 8)))
    ranks = draw_ranks(jax.random.fold_in(key_of[4], 71), 0)
    return {"diag_coords": diag_coords, "panel_coords": panel_coords, "test_matrix": test_matrix, "ranks": ranks}


range_length = 409.6
nugget = 0.5
shift_ratio = 0.01

def matern(first, second):
    delta_x = (first[0][:, None] - second[0][None, :]).astype(jnp.float32)
    delta_y = (first[1][:, None] - second[1][None, :]).astype(jnp.float32)
    return jnp.exp(-jnp.sqrt(delta_x * delta_x + delta_y * delta_y) / range_length)

def reference(diag_coords, panel_coords, test_matrix, ranks):
    cov = matern(diag_coords, diag_coords) + nugget * jnp.eye(NB, dtype=jnp.float32)
    lower = jnp.linalg.cholesky(cov)
    columns = jnp.arange(R, dtype=jnp.int32)
    masks = (columns[None, :] < ranks[:, None]).astype(jnp.bfloat16)
    tests = test_matrix * masks[:, None, :]

    def panel_tile(inputs):
        points, test, mask, rank = inputs
        block = matern(points, diag_coords)
        solved = jax.scipy.linalg.solve_triangular(lower, block.T, lower=True).T
        sample = jnp.dot(solved, test.astype(jnp.float32), precision=lax.Precision.HIGHEST)
        gram = jnp.dot(sample.T, sample, precision=lax.Precision.HIGHEST)
        maskf = mask.astype(jnp.float32)
        shift = shift_ratio * jnp.sum(jnp.diagonal(gram)) / rank.astype(jnp.float32)
        shifted = gram + jnp.diag(shift * maskf + 1.0 - maskf)
        factor = jnp.linalg.cholesky(shifted)
        basis = jax.scipy.linalg.solve_triangular(factor, sample.T, lower=True).T
        basis = basis.astype(jnp.bfloat16)
        coeff = jnp.dot(solved.T, basis.astype(jnp.float32), precision=lax.Precision.HIGHEST)
        return (basis, coeff.astype(jnp.bfloat16))
    left, coeff = lax.map(panel_tile, (jnp.transpose(panel_coords, (1, 0, 2)), tests, masks, ranks))

    def update_row(coeff_row):
        core = jnp.einsum('nr,jns->jrs', coeff_row.astype(jnp.float32), coeff.astype(jnp.float32))
        core = core.astype(jnp.bfloat16)
        return jnp.einsum('jns,jrs->jnr', left.astype(jnp.float32), core.astype(jnp.float32)).astype(jnp.bfloat16)
    update = lax.map(update_row, coeff)
    return (left, update)
```

```python
import functools

import jax
import jax.numpy as jnp
from jax import lax
from jax.experimental import pallas as pl
from jax.experimental.pallas import tpu as pltpu
from jax.sharding import PartitionSpec as P

range_length = 409.6
nugget = 0.5
shift_ratio = 0.01
BLOCK = 128
SUB = 8


def matern(first, second):
    delta_x = (first[0][:, None] - second[0][None, :]).astype(jnp.float32)
    delta_y = (first[1][:, None] - second[1][None, :]).astype(jnp.float32)
    return jnp.exp(-jnp.sqrt(delta_x * delta_x + delta_y * delta_y) / range_length)


def split(value):
    high = value.astype(jnp.bfloat16)
    low = (value - high.astype(jnp.float32)).astype(jnp.bfloat16)
    return high, low


def contract_rows(first, second):
    return lax.dot_general(first, second, (((0,), (0,)), ((), ())), preferred_element_type=jnp.float32)


def leaf(work):
    lane = lax.broadcasted_iota(jnp.int32, (SUB, BLOCK), 1)
    sub = lax.broadcasted_iota(jnp.int32, (SUB, BLOCK), 0)
    for panel in range(BLOCK // SUB):
        start = panel * SUB
        end = start + SUB
        rows = work[start:end, :]
        columns = [jnp.broadcast_to(rows[:, start + j : start + j + 1], (SUB, BLOCK)) for j in range(SUB)]
        inside = (lane >= start) & (lane < end)
        rows = jnp.where(inside, (lane - start == sub).astype(jnp.float32), rows)
        pivots = jnp.ones((SUB, BLOCK), jnp.float32)
        for k in range(SUB):
            pivot = jnp.broadcast_to(columns[k][k : k + 1, :], (SUB, BLOCK))
            pivots = jnp.where(sub == k, pivot, pivots)
            if k == SUB - 1:
                break
            factor = jnp.where(sub > k, columns[k] * (1.0 / pivot), 0.0)
            rows = rows - factor * rows[k : k + 1, :]
            for j in range(k + 1, SUB):
                columns[j] = columns[j] - factor * columns[j][k : k + 1, :]
        rows = rows * lax.rsqrt(pivots)
        work[start:end, :] = rows
        if end < BLOCK:
            right = jnp.where(lane >= end, rows, 0.0)
            change = lax.dot_general(
                right, rows, (((0,), (0,)), ((), ())),
                precision=lax.Precision.HIGHEST, preferred_element_type=jnp.float32,
            )
            below = work[end:, :]
            lanes = lax.broadcasted_iota(jnp.int32, below.shape, 1)
            below = jnp.where((lanes >= start) & (lanes < end), 0.0, below)
            work[end:, :] = below - change[end:, :]


def factor_kernel(a_ref, out_ref, work, left, right):
    size = a_ref.shape[0]
    blocks = size // BLOCK

    @pl.loop(0, blocks)
    def _(i):
        at = pl.ds(pl.multiple_of(i * BLOCK, BLOCK), BLOCK)
        out_ref[at, :] = a_ref[at, :]

    @pl.loop(0, blocks)
    def _(k):
        start = pl.multiple_of(k * BLOCK, BLOCK)
        at = pl.ds(start, BLOCK)
        work[...] = out_ref[at, at]
        leaf(work)
        row = lax.broadcasted_iota(jnp.int32, (BLOCK, BLOCK), 0)
        col = lax.broadcasted_iota(jnp.int32, (BLOCK, BLOCK), 1)
        inverse = jnp.where(row >= col, work[...], 0.0)
        high, low = split(inverse)
        both = jnp.concatenate([high, high, low], axis=1)
        p_high, p_low = split(out_ref[at, :])
        stacked = jnp.concatenate([p_high, p_low, p_high], axis=0)
        panel = jnp.dot(both, stacked, preferred_element_type=jnp.float32)
        wide = lax.broadcasted_iota(jnp.int32, (BLOCK, size), 1)
        out_ref[at, :] = jnp.where(wide < start, panel, 0.0)
        out_ref[at, at] = inverse
        r_high, r_low = split(panel)
        left[0:BLOCK, :] = r_high
        left[BLOCK : 2 * BLOCK, :] = r_high
        left[2 * BLOCK :, :] = r_low
        right[0:BLOCK, :] = r_high
        right[BLOCK : 2 * BLOCK, :] = r_low
        right[2 * BLOCK :, :] = r_high
        right[0:BLOCK, at] = high
        right[BLOCK : 2 * BLOCK, at] = low
        right[2 * BLOCK :, at] = high

        @pl.loop(k + 1, blocks)
        def _(i):
            rows = pl.ds(pl.multiple_of(i * BLOCK, BLOCK), BLOCK)
            out_ref[rows, at] = jnp.zeros((BLOCK, BLOCK), jnp.float32)
            out_ref[rows, :] = out_ref[rows, :] - contract_rows(left[:, rows], right[...])


def inverse_factor(matrix):
    size = matrix.shape[0]
    return pl.pallas_call(
        factor_kernel,
        out_shape=jax.ShapeDtypeStruct((size, size), jnp.float32),
        in_specs=[pl.BlockSpec(memory_space=pltpu.VMEM)],
        out_specs=pl.BlockSpec(memory_space=pltpu.VMEM),
        scratch_shapes=[
            pltpu.VMEM((BLOCK, BLOCK), jnp.float32),
            pltpu.VMEM((3 * BLOCK, size), jnp.bfloat16),
            pltpu.VMEM((3 * BLOCK, size), jnp.bfloat16),
        ],
        compiler_params=pltpu.CompilerParams(vmem_limit_bytes=48 * 1024 * 1024),
        cost_estimate=pl.CostEstimate(
            flops=size * 400000 + 6 * size**3, bytes_accessed=8 * size * size, transcendentals=0
        ),
    )(matrix)


def high_dot(spec, first, second):
    return jnp.einsum(spec, first, second, precision=lax.Precision.HIGH, preferred_element_type=jnp.float32)


def spread(value, n_row, n_col, row_tiles, row_index, col_index):
    root = col_index // row_tiles
    reached = n_row
    step = n_row // 2
    while step >= 1:
        pairs = []
        for b in range(n_col):
            source = b // row_tiles
            for a in range(n_row):
                if (a ^ source) % reached == 0:
                    pairs.append((a * n_col + b, (a ^ step) * n_col + b))
        moved = lax.ppermute(value, ("row", "col"), pairs)
        gets = ((row_index ^ root) % reached) == step
        value = jnp.where(gets, moved, value)
        reached = step
        step //= 2
    return value


def shards(diag_coords, panel_coords, test_matrix, ranks):
    points = diag_coords.shape[1]
    row_tiles = panel_coords.shape[1]
    width = test_matrix.shape[2]
    share = test_matrix.shape[1]
    n_row = lax.axis_size("row")
    n_col = lax.axis_size("col")
    row_index = lax.axis_index("row")
    col_index = lax.axis_index("col")
    own = col_index % row_tiles
    tile = row_index * row_tiles + own

    all_points = lax.all_gather(panel_coords, "col", axis=2, tiled=True)
    all_tests = lax.all_gather(test_matrix, "col", axis=1, tiled=True)
    cov = matern(diag_coords, diag_coords) + nugget * jnp.eye(points, dtype=jnp.float32)
    lower_inverse = inverse_factor(cov)

    columns = jnp.arange(width, dtype=jnp.int32)
    rank = lax.dynamic_index_in_dim(ranks, tile, 0, keepdims=False)
    mask = (columns < rank).astype(jnp.float32)
    tests = lax.dynamic_index_in_dim(all_tests, own, 0, keepdims=False)
    tests = tests * mask.astype(jnp.bfloat16)[None, :]
    tile_points = lax.dynamic_index_in_dim(all_points, own, 1, keepdims=False)
    block = matern(tile_points, diag_coords)

    weights = high_dot("mk,mr->kr", lower_inverse, tests.astype(jnp.float32))
    sample = high_dot("nk,kr->nr", block, weights)
    gram = high_dot("nr,ns->rs", sample, sample)
    shift = shift_ratio * jnp.trace(gram) / rank.astype(jnp.float32)
    shifted = gram + jnp.diag(shift * mask + 1.0 - mask)
    factor_inverse = inverse_factor(shifted)
    basis = high_dot("nr,sr->ns", sample, factor_inverse).astype(jnp.bfloat16)
    projected = high_dot("nm,nr->mr", block, basis.astype(jnp.float32))
    coeff = high_dot("km,mr->kr", lower_inverse, projected).astype(jnp.bfloat16)

    both = spread(jnp.stack([basis, coeff]), n_row, n_col, row_tiles, row_index, col_index)
    pieces = basis.reshape(n_col, share, width)
    lefts, coeffs = [], []
    for step in range(row_tiles):
        if step == 0:
            lefts.append(lax.dynamic_index_in_dim(pieces, col_index, 0, keepdims=False))
            coeffs.append(coeff)
            continue
        target = [b // row_tiles * row_tiles + (b - step) % row_tiles for b in range(n_col)]
        pairs = [(b, target[b]) for b in range(n_col)]
        to = col_index // row_tiles * row_tiles + (col_index - step) % row_tiles
        coeffs.append(lax.ppermute(coeff, "col", pairs))
        lefts.append(lax.ppermute(lax.dynamic_index_in_dim(pieces, to, 0, keepdims=False), "col", pairs))
    def ordered(entries):
        stack = jnp.stack(entries)
        return jnp.roll(stack, own, axis=0) if row_tiles > 1 else stack

    left = ordered(lefts)
    row_coeff = ordered(coeffs)
    col_left, col_coeff = both[0], both[1]
    core = jnp.einsum("inr,ns->irs", row_coeff, col_coeff, preferred_element_type=jnp.float32)
    core = core.astype(jnp.bfloat16)
    update = jnp.einsum("ns,irs->inr", col_left, core, preferred_element_type=jnp.float32)
    return (left, update.astype(jnp.bfloat16)[:, None])


def solution(mesh):
    in_specs = (P(), P(None, "row", "col"), P("row", "col", None), P())
    out_specs = (P("row", "col", None), P("row", "col", None, None))
    return jax.shard_map(shards, mesh=mesh, in_specs=in_specs, out_specs=out_specs, check_vma=False)
```

```python
import functools

import jax
import jax.numpy as jnp
from jax import lax
from jax.experimental import pallas as pl
from jax.experimental.pallas import tpu as pltpu
from jax.sharding import PartitionSpec as P

range_length = 409.6
nugget = 0.5
shift_ratio = 0.01
BLOCK = 128
SUB = 8


def matern(first, second):
    delta_x = (first[0][:, None] - second[0][None, :]).astype(jnp.float32)
    delta_y = (first[1][:, None] - second[1][None, :]).astype(jnp.float32)
    return jnp.exp(-jnp.sqrt(delta_x * delta_x + delta_y * delta_y) / range_length)


def split(value):
    high = value.astype(jnp.bfloat16)
    low = (value - high.astype(jnp.float32)).astype(jnp.bfloat16)
    return high, low


def contract_rows(first, second):
    return lax.dot_general(first, second, (((0,), (0,)), ((), ())), preferred_element_type=jnp.float32)


def leaf(work):
    lane = lax.broadcasted_iota(jnp.int32, (SUB, BLOCK), 1)
    sub = lax.broadcasted_iota(jnp.int32, (SUB, BLOCK), 0)
    for panel in range(BLOCK // SUB):
        start = panel * SUB
        end = start + SUB
        spots = [at for at in (start, end, end + SUB) if at < BLOCK]
        loaded = [work[at : at + SUB, :] for at in spots]
        inside = (lane >= start) & (lane < end)
        columns = [
            [jnp.broadcast_to(part[:, start + j : start + j + 1], (SUB, BLOCK)) for j in range(SUB)]
            for part in loaded
        ]
        own = (lane - start == sub).astype(jnp.float32)
        rows = [jnp.where(inside, own if g == 0 else 0.0, part) for g, part in enumerate(loaded)]
        pivots = jnp.ones((SUB, BLOCK), jnp.float32)
        for k in range(SUB):
            pivot = jnp.broadcast_to(columns[0][k][k : k + 1, :], (SUB, BLOCK))
            pivots = jnp.where(sub == k, pivot, pivots)
            ratio = 1.0 / pivot
            factors = [part[k] * ratio for part in columns]
            factors[0] = jnp.where(sub > k, factors[0], 0.0)
            top = rows[0][k : k + 1, :]
            rows = [part - factor * top for part, factor in zip(rows, factors)]
            for j in range(k + 1, SUB):
                entry = columns[0][j][k : k + 1, :]
                for part, factor in zip(columns, factors):
                    part[j] = part[j] - factor * entry
        scaled = rows[0] * lax.rsqrt(pivots)
        work[start:end, :] = scaled
        for at, part in zip(spots[1:], rows[1:]):
            work[at : at + SUB, :] = part
        rest = end + 2 * SUB
        if rest < BLOCK:
            right = jnp.where(lane >= rest, scaled, 0.0)
            change = lax.dot_general(
                right, scaled, (((0,), (0,)), ((), ())),
                precision=lax.Precision.HIGHEST, preferred_element_type=jnp.float32,
            )
            below = work[rest:, :]
            lanes = lax.broadcasted_iota(jnp.int32, below.shape, 1)
            below = jnp.where((lanes >= start) & (lanes < end), 0.0, below)
            work[rest:, :] = below - change[rest:, :]


def factor_kernel(a_ref, out_ref, work, left, right):
    size = a_ref.shape[0]
    blocks = size // BLOCK

    @pl.loop(0, blocks)
    def _(i):
        at = pl.ds(pl.multiple_of(i * BLOCK, BLOCK), BLOCK)
        out_ref[at, :] = a_ref[at, :]

    @pl.loop(0, blocks)
    def _(k):
        start = pl.multiple_of(k * BLOCK, BLOCK)
        at = pl.ds(start, BLOCK)
        work[...] = out_ref[at, at]
        leaf(work)
        row = lax.broadcasted_iota(jnp.int32, (BLOCK, BLOCK), 0)
        col = lax.broadcasted_iota(jnp.int32, (BLOCK, BLOCK), 1)
        inverse = jnp.where(row >= col, work[...], 0.0)
        high, low = split(inverse)
        both = jnp.concatenate([high, high, low], axis=1)
        p_high, p_low = split(out_ref[at, :])
        stacked = jnp.concatenate([p_high, p_low, p_high], axis=0)
        panel = jnp.dot(both, stacked, preferred_element_type=jnp.float32)
        wide = lax.broadcasted_iota(jnp.int32, (BLOCK, size), 1)
        out_ref[at, :] = jnp.where(wide < start, panel, 0.0)
        out_ref[at, at] = inverse
        r_high, r_low = split(panel)
        left[0:BLOCK, :] = r_high
        left[BLOCK : 2 * BLOCK, :] = r_high
        left[2 * BLOCK :, :] = r_low
        right[0:BLOCK, :] = r_high
        right[BLOCK : 2 * BLOCK, :] = r_low
        right[2 * BLOCK :, :] = r_high
        right[0:BLOCK, at] = high
        right[BLOCK : 2 * BLOCK, at] = low
        right[2 * BLOCK :, at] = high

        def update(first, count):
            rows = pl.ds(pl.multiple_of(first * BLOCK, BLOCK), count * BLOCK)
            out_ref[rows, at] = jnp.zeros((count * BLOCK, BLOCK), jnp.float32)
            out_ref[rows, :] = out_ref[rows, :] - contract_rows(left[:, rows], right[...])

        rest = blocks - 1 - k

        @pl.loop(0, rest // 2)
        def _(pair):
            update(k + 1 + 2 * pair, 2)

        @pl.when(rest % 2 == 1)
        def _():
            update(blocks - 1, 1)


def inverse_factor(matrix):
    size = matrix.shape[0]
    return pl.pallas_call(
        factor_kernel,
        out_shape=jax.ShapeDtypeStruct((size, size), jnp.float32),
        in_specs=[pl.BlockSpec(memory_space=pltpu.VMEM)],
        out_specs=pl.BlockSpec(memory_space=pltpu.VMEM),
        scratch_shapes=[
            pltpu.VMEM((BLOCK, BLOCK), jnp.float32),
            pltpu.VMEM((3 * BLOCK, size), jnp.bfloat16),
            pltpu.VMEM((3 * BLOCK, size), jnp.bfloat16),
        ],
        compiler_params=pltpu.CompilerParams(vmem_limit_bytes=48 * 1024 * 1024),
        cost_estimate=pl.CostEstimate(
            flops=size * 400000 + 6 * size**3, bytes_accessed=8 * size * size, transcendentals=0
        ),
    )(matrix)


def high_dot(spec, first, second):
    return jnp.einsum(spec, first, second, precision=lax.Precision.HIGH, preferred_element_type=jnp.float32)


def spread(value, n_row, n_col, row_tiles, row_index, col_index):
    root = col_index // row_tiles
    reached = n_row
    step = n_row // 2
    while step >= 1:
        pairs = []
        for b in range(n_col):
            source = b // row_tiles
            for a in range(n_row):
                if (a ^ source) % reached == 0:
                    pairs.append((a * n_col + b, (a ^ step) * n_col + b))
        moved = lax.ppermute(value, ("row", "col"), pairs)
        gets = ((row_index ^ root) % reached) == step
        value = jnp.where(gets, moved, value)
        reached = step
        step //= 2
    return value


def shards(diag_coords, panel_coords, test_matrix, ranks):
    points = diag_coords.shape[1]
    row_tiles = panel_coords.shape[1]
    width = test_matrix.shape[2]
    share = test_matrix.shape[1]
    n_row = lax.axis_size("row")
    n_col = lax.axis_size("col")
    row_index = lax.axis_index("row")
    col_index = lax.axis_index("col")
    own = col_index % row_tiles
    tile = row_index * row_tiles + own

    halves = jnp.stack(
        [panel_coords[0] // 256, panel_coords[0] % 256, panel_coords[1] // 256, panel_coords[1] % 256], axis=-1
    ).astype(jnp.bfloat16)
    halves = jnp.pad(halves, ((0, 0), (0, 0), (0, 128 - 4)))
    gathered = lax.all_gather(jnp.concatenate([test_matrix, halves], axis=2), "col", axis=1, tiled=True)
    cov = matern(diag_coords, diag_coords) + nugget * jnp.eye(points, dtype=jnp.float32)
    lower_inverse = inverse_factor(cov)

    columns = jnp.arange(width, dtype=jnp.int32)
    rank = lax.dynamic_index_in_dim(ranks, tile, 0, keepdims=False)
    mask = (columns < rank).astype(jnp.float32)
    mine = lax.dynamic_index_in_dim(gathered, own, 0, keepdims=False)
    tests = mine[:, :width] * mask.astype(jnp.bfloat16)[None, :]
    halves = mine[:, width : width + 4].astype(jnp.float32)
    tile_x = halves[:, 0:1] * 256.0 + halves[:, 1:2]
    tile_y = halves[:, 2:3] * 256.0 + halves[:, 3:4]
    delta_x = tile_x - diag_coords[0].astype(jnp.float32)[None, :]
    delta_y = tile_y - diag_coords[1].astype(jnp.float32)[None, :]
    block = jnp.exp(-jnp.sqrt(delta_x * delta_x + delta_y * delta_y) / range_length)

    weights = high_dot("mk,mr->kr", lower_inverse, tests.astype(jnp.float32))
    sample = high_dot("nk,kr->nr", block, weights)
    gram = high_dot("nr,ns->rs", sample, sample)
    shift = shift_ratio * jnp.trace(gram) / rank.astype(jnp.float32)
    shifted = gram + jnp.diag(shift * mask + 1.0 - mask)
    factor_inverse = inverse_factor(shifted)
    basis = high_dot("nr,sr->ns", sample, factor_inverse).astype(jnp.bfloat16)
    pieces = basis.reshape(n_col, share, width)
    group = col_index // row_tiles * row_tiles

    def shifted_pairs(step):
        return [(b, b // row_tiles * row_tiles + (b - step) % row_tiles) for b in range(n_col)]

    lefts = [lax.dynamic_index_in_dim(pieces, col_index, 0, keepdims=False)]
    for step in range(1, row_tiles):
        to = group + (col_index - step) % row_tiles
        piece = lax.dynamic_index_in_dim(pieces, to, 0, keepdims=False)
        lefts.append(lax.ppermute(piece, "col", shifted_pairs(step)))
    col_left = spread(basis, n_row, n_col, row_tiles, row_index, col_index)

    projected = high_dot("nm,nr->mr", block, basis.astype(jnp.float32))
    coeff = high_dot("km,mr->kr", lower_inverse, projected).astype(jnp.bfloat16)
    coeffs = [coeff] + [lax.ppermute(coeff, "col", shifted_pairs(step)) for step in range(1, row_tiles)]
    col_coeff = spread(coeff, n_row, n_col, row_tiles, row_index, col_index)

    def ordered(entries):
        stack = jnp.stack(entries)
        return jnp.roll(stack, own, axis=0) if row_tiles > 1 else stack

    left = ordered(lefts)
    row_coeff = ordered(coeffs)
    core = jnp.einsum("inr,ns->irs", row_coeff, col_coeff, preferred_element_type=jnp.float32)
    core = core.astype(jnp.bfloat16)
    many_left = jnp.broadcast_to(col_left[None], (row_tiles,) + col_left.shape)
    update = jnp.einsum("ins,irs->inr", many_left, core, preferred_element_type=jnp.float32)
    return (left, update.astype(jnp.bfloat16)[:, None])


def solution(mesh):
    in_specs = (P(), P(None, "row", "col"), P("row", "col", None), P())
    out_specs = (P("row", "col", None), P("row", "col", None, None))
    return jax.shard_map(shards, mesh=mesh, in_specs=in_specs, out_specs=out_specs, check_vma=False)
```

```python
import functools

import jax
import jax.numpy as jnp
from jax import lax
from jax.experimental import pallas as pl
from jax.experimental.pallas import tpu as pltpu
from jax.sharding import PartitionSpec as P

range_length = 409.6
nugget = 0.5
shift_ratio = 0.01
BLOCK = 128
SUB = 8


def split(value):
    high = value.astype(jnp.bfloat16)
    low = (value - high.astype(jnp.float32)).astype(jnp.bfloat16)
    return high, low


def contract_rows(first, second):
    return lax.dot_general(first, second, (((0,), (0,)), ((), ())), preferred_element_type=jnp.float32)


def leaf(work):
    lane = lax.broadcasted_iota(jnp.int32, (SUB, BLOCK), 1)
    sub = lax.broadcasted_iota(jnp.int32, (SUB, BLOCK), 0)
    for panel in range(BLOCK // SUB):
        start = panel * SUB
        end = start + SUB
        spots = [at for at in (start, end, end + SUB) if at < BLOCK]
        loaded = [work[at : at + SUB, :] for at in spots]
        inside = (lane >= start) & (lane < end)
        columns = [
            [jnp.broadcast_to(part[:, start + j : start + j + 1], (SUB, BLOCK)) for j in range(SUB)]
            for part in loaded
        ]
        own = (lane - start == sub).astype(jnp.float32)
        rows = [jnp.where(inside, own if g == 0 else 0.0, part) for g, part in enumerate(loaded)]
        pivots = jnp.ones((SUB, BLOCK), jnp.float32)
        for k in range(SUB):
            pivot = jnp.broadcast_to(columns[0][k][k : k + 1, :], (SUB, BLOCK))
            pivots = jnp.where(sub == k, pivot, pivots)
            ratio = 1.0 / pivot
            factors = [part[k] * ratio for part in columns]
            factors[0] = jnp.where(sub > k, factors[0], 0.0)
            top = rows[0][k : k + 1, :]
            rows = [part - factor * top for part, factor in zip(rows, factors)]
            for j in range(k + 1, SUB):
                entry = columns[0][j][k : k + 1, :]
                for part, factor in zip(columns, factors):
                    part[j] = part[j] - factor * entry
        scaled = rows[0] * lax.rsqrt(pivots)
        work[start:end, :] = scaled
        for at, part in zip(spots[1:], rows[1:]):
            work[at : at + SUB, :] = part
        rest = end + 2 * SUB
        if rest < BLOCK:
            right = jnp.where(lane >= rest, scaled, 0.0)
            change = lax.dot_general(
                right, scaled, (((0,), (0,)), ((), ())),
                precision=lax.Precision.HIGHEST, preferred_element_type=jnp.float32,
            )
            below = work[rest:, :]
            lanes = lax.broadcasted_iota(jnp.int32, below.shape, 1)
            below = jnp.where((lanes >= start) & (lanes < end), 0.0, below)
            work[rest:, :] = below - change[rest:, :]


def load_matrix(a_ref, out_ref):
    @pl.loop(0, out_ref.shape[0] // BLOCK)
    def _(i):
        at = pl.ds(pl.multiple_of(i * BLOCK, BLOCK), BLOCK)
        out_ref[at, :] = a_ref[at, :]


def load_covariance(down_ref, across_ref, out_ref):
    size = out_ref.shape[0]
    chunk = 4 * BLOCK if size % (4 * BLOCK) == 0 else BLOCK

    @pl.loop(0, size // BLOCK)
    def _(i):
        first = pl.multiple_of(i * BLOCK, BLOCK)
        at = pl.ds(first, BLOCK)
        for start in range(0, size, chunk):

            @pl.when(start + chunk > first)
            def _():
                delta_x = down_ref[at, 0:1] - across_ref[0:1, start : start + chunk]
                delta_y = down_ref[at, 1:2] - across_ref[1:2, start : start + chunk]
                value = jnp.exp(-jnp.sqrt(delta_x * delta_x + delta_y * delta_y) * (1.0 / range_length))
                row = lax.broadcasted_iota(jnp.int32, value.shape, 0) + first
                col = lax.broadcasted_iota(jnp.int32, value.shape, 1) + start
                out_ref[at, start : start + chunk] = value + jnp.where(row == col, nugget, 0.0)


def factor_kernel(load, *refs):
    *sources, out_ref, work, left, right = refs
    size = out_ref.shape[0]
    blocks = size // BLOCK
    load(*sources, out_ref)

    @pl.loop(0, blocks)
    def _(k):
        start = pl.multiple_of(k * BLOCK, BLOCK)
        at = pl.ds(start, BLOCK)
        work[...] = out_ref[at, at]
        leaf(work)
        row = lax.broadcasted_iota(jnp.int32, (BLOCK, BLOCK), 0)
        col = lax.broadcasted_iota(jnp.int32, (BLOCK, BLOCK), 1)
        inverse = jnp.where(row >= col, work[...], 0.0)
        high, low = split(inverse)
        both = jnp.concatenate([high, high, low], axis=1)
        p_high, p_low = split(out_ref[at, :])
        stacked = jnp.concatenate([p_high, p_low, p_high], axis=0)
        panel = jnp.dot(both, stacked, preferred_element_type=jnp.float32)
        wide = lax.broadcasted_iota(jnp.int32, (BLOCK, size), 1)
        out_ref[at, :] = jnp.where(wide < start, panel, 0.0)
        out_ref[at, at] = inverse
        r_high, r_low = split(panel)
        left[0:BLOCK, :] = r_high
        left[BLOCK : 2 * BLOCK, :] = r_high
        left[2 * BLOCK :, :] = r_low
        right[0:BLOCK, :] = r_high
        right[BLOCK : 2 * BLOCK, :] = r_low
        right[2 * BLOCK :, :] = r_high
        right[0:BLOCK, at] = high
        right[BLOCK : 2 * BLOCK, at] = low
        right[2 * BLOCK :, at] = high

        def update(first, count):
            rows = pl.ds(pl.multiple_of(first * BLOCK, BLOCK), count * BLOCK)
            out_ref[rows, at] = jnp.zeros((count * BLOCK, BLOCK), jnp.float32)
            out_ref[rows, :] = out_ref[rows, :] - contract_rows(left[:, rows], right[...])

        rest = blocks - 1 - k

        @pl.loop(0, rest // 2)
        def _(pair):
            update(k + 1 + 2 * pair, 2)

        @pl.when(rest % 2 == 1)
        def _():
            update(blocks - 1, 1)


def inverse_factor(load, size, *sources):
    return pl.pallas_call(
        functools.partial(factor_kernel, load),
        out_shape=jax.ShapeDtypeStruct((size, size), jnp.float32),
        in_specs=[pl.BlockSpec(memory_space=pltpu.VMEM)] * len(sources),
        out_specs=pl.BlockSpec(memory_space=pltpu.VMEM),
        scratch_shapes=[
            pltpu.VMEM((BLOCK, BLOCK), jnp.float32),
            pltpu.VMEM((3 * BLOCK, size), jnp.bfloat16),
            pltpu.VMEM((3 * BLOCK, size), jnp.bfloat16),
        ],
        compiler_params=pltpu.CompilerParams(vmem_limit_bytes=48 * 1024 * 1024),
        cost_estimate=pl.CostEstimate(
            flops=size * 400000 + 6 * size**3, bytes_accessed=8 * size * size, transcendentals=0
        ),
    )(*sources)


def high_dot(spec, first, second):
    return jnp.einsum(spec, first, second, precision=lax.Precision.HIGH, preferred_element_type=jnp.float32)


def spread(value, n_row, n_col, row_tiles, row_index, col_index):
    root = col_index // row_tiles
    reached = n_row
    step = n_row // 2
    while step >= 1:
        pairs = []
        for b in range(n_col):
            source = b // row_tiles
            for a in range(n_row):
                if (a ^ source) % reached == 0:
                    pairs.append((a * n_col + b, (a ^ step) * n_col + b))
        moved = lax.ppermute(value, ("row", "col"), pairs)
        gets = ((row_index ^ root) % reached) == step
        value = jnp.where(gets, moved, value)
        reached = step
        step //= 2
    return value


def shards(diag_coords, panel_coords, test_matrix, ranks):
    points = diag_coords.shape[1]
    row_tiles = panel_coords.shape[1]
    width = test_matrix.shape[2]
    share = test_matrix.shape[1]
    n_row = lax.axis_size("row")
    n_col = lax.axis_size("col")
    assert row_tiles in (1, 2) and n_col == n_row * row_tiles and n_col % 4 == 0
    row_index = lax.axis_index("row")
    col_index = lax.axis_index("col")
    own = (col_index ^ (col_index // 2) ^ row_index) % row_tiles
    tile = row_index * row_tiles + own

    halves = jnp.stack(
        [panel_coords[0] // 256, panel_coords[0] % 256, panel_coords[1] // 256, panel_coords[1] % 256], axis=-1
    ).astype(jnp.bfloat16)
    halves = jnp.pad(halves, ((0, 0), (0, 0), (0, 128 - 4)))
    gathered = lax.all_gather(jnp.concatenate([test_matrix, halves], axis=2), "col", axis=1, tiled=True)
    across = diag_coords.astype(jnp.float32)
    lower_inverse = inverse_factor(load_covariance, points, across.T, across)

    columns = jnp.arange(width, dtype=jnp.int32)
    rank = lax.dynamic_index_in_dim(ranks, tile, 0, keepdims=False)
    mask = (columns < rank).astype(jnp.float32)
    mine = lax.dynamic_index_in_dim(gathered, own, 0, keepdims=False)
    tests = mine[:, :width] * mask.astype(jnp.bfloat16)[None, :]
    halves = mine[:, width : width + 4].astype(jnp.float32)
    tile_x = halves[:, 0:1] * 256.0 + halves[:, 1:2]
    tile_y = halves[:, 2:3] * 256.0 + halves[:, 3:4]
    delta_x = tile_x - across[0][None, :]
    delta_y = tile_y - across[1][None, :]
    block = jnp.exp(-jnp.sqrt(delta_x * delta_x + delta_y * delta_y) / range_length)

    weights = high_dot("mk,mr->kr", lower_inverse, tests.astype(jnp.float32))
    sample = high_dot("nk,kr->nr", block, weights)
    gram = high_dot("nr,ns->rs", sample, sample)
    shift = shift_ratio * jnp.sum(sample * sample) / rank.astype(jnp.float32)
    shifted = gram + jnp.diag(shift * mask + 1.0 - mask)
    factor_inverse = inverse_factor(load_matrix, width, shifted)
    basis = high_dot("nr,sr->ns", sample, factor_inverse).astype(jnp.bfloat16)
    pieces = basis.reshape(n_col, share, width)

    def swap(value, distance):
        return lax.ppermute(value, "col", [(b, b ^ distance) for b in range(n_col)])

    lefts = [lax.dynamic_index_in_dim(pieces, col_index, 0, keepdims=False)]
    if row_tiles > 1:
        lefts.append(swap(lax.dynamic_index_in_dim(pieces, col_index ^ 1, 0, keepdims=False), 1))
    col_left = spread(basis, n_row, n_col, row_tiles, row_index, col_index)

    projected = high_dot("nm,nr->mr", block, basis.astype(jnp.float32))
    half = points // 2
    upper = high_dot("km,mr->kr", lower_inverse[:half, :half], projected[:half]).astype(jnp.bfloat16)
    lower = high_dot("km,mr->kr", lower_inverse[half:], projected).astype(jnp.bfloat16)
    coeff = jnp.concatenate([upper, lower])
    coeffs = [coeff]
    if row_tiles > 1:
        coeffs.append(jnp.concatenate([swap(upper, 1), swap(lower, 2)]))
    col_coeff = spread(coeff, n_row, n_col, row_tiles, row_index, col_index)

    def ordered(entries):
        stack = jnp.stack(entries)
        return jnp.roll(stack, own, axis=0) if row_tiles > 1 else stack

    left = ordered(lefts)
    row_coeff = ordered(coeffs)
    core = jnp.einsum("inr,ns->irs", row_coeff, col_coeff, preferred_element_type=jnp.float32)
    core = core.astype(jnp.bfloat16)
    many_left = jnp.broadcast_to(col_left[None], (row_tiles,) + col_left.shape)
    update = jnp.einsum("ins,irs->inr", many_left, core, preferred_element_type=jnp.float32)
    return (left, update.astype(jnp.bfloat16)[:, None])


def solution(mesh):
    in_specs = (P(), P(None, "row", "col"), P("row", "col", None), P())
    out_specs = (P("row", "col", None), P("row", "col", None, None))
    return jax.shard_map(shards, mesh=mesh, in_specs=in_specs, out_specs=out_specs, check_vma=False)
```

```python
import functools

import jax
import jax.numpy as jnp
from jax import lax
from jax.experimental import pallas as pl
from jax.experimental.pallas import tpu as pltpu
from jax.sharding import PartitionSpec as P

range_length = 409.6
nugget = 0.5
shift_ratio = 0.01
BLOCK = 128
SUB = 8


def split(value):
    high = value.astype(jnp.bfloat16)
    low = (value - high.astype(jnp.float32)).astype(jnp.bfloat16)
    return high, low


def contract_rows(first, second):
    return lax.dot_general(first, second, (((0,), (0,)), ((), ())), preferred_element_type=jnp.float32)


def leaf(work):
    lane = lax.broadcasted_iota(jnp.int32, (SUB, BLOCK), 1)
    sub = lax.broadcasted_iota(jnp.int32, (SUB, BLOCK), 0)
    for panel in range(BLOCK // SUB):
        start = panel * SUB
        end = start + SUB
        spots = [at for at in (start, end, end + SUB) if at < BLOCK]
        loaded = [work[at : at + SUB, :] for at in spots]
        inside = (lane >= start) & (lane < end)
        columns = [
            [jnp.broadcast_to(part[:, start + j : start + j + 1], (SUB, BLOCK)) for j in range(SUB)]
            for part in loaded
        ]
        own = (lane - start == sub).astype(jnp.float32)
        rows = [jnp.where(inside, own if g == 0 else 0.0, part) for g, part in enumerate(loaded)]
        pivots = jnp.ones((SUB, BLOCK), jnp.float32)
        corner = {
            (i, j): jnp.broadcast_to(columns[0][j][i : i + 1, :], (SUB, BLOCK)) for j in range(SUB) for i in range(j, SUB)
        }
        for k in range(SUB):
            pivot = corner[k, k]
            pivots = jnp.where(sub == k, pivot, pivots)
            ratio = pl.reciprocal(pivot, approx=True)
            ratio = ratio * (2.0 - pivot * ratio)
            unit = {j: corner[j, k] * ratio for j in range(k + 1, SUB)}
            for j in range(k + 1, SUB):
                for i in range(j, SUB):
                    corner[i, j] = corner[i, j] - corner[i, k] * unit[j]
            factors = [part[k] * ratio for part in columns]
            factors[0] = jnp.where(sub > k, factors[0], 0.0)
            top = rows[0][k : k + 1, :]
            rows = [part - factor * top for part, factor in zip(rows, factors)]
            for part in columns:
                for j in range(k + 1, SUB):
                    part[j] = part[j] - part[k] * unit[j]
        scaled = rows[0] * lax.rsqrt(pivots)
        work[start:end, :] = scaled
        for at, part in zip(spots[1:], rows[1:]):
            work[at : at + SUB, :] = part
        rest = end + 2 * SUB
        if rest < BLOCK:
            right = jnp.where(lane >= rest, scaled, 0.0)
            change = lax.dot_general(
                right, scaled, (((0,), (0,)), ((), ())),
                precision=lax.Precision.HIGHEST, preferred_element_type=jnp.float32,
            )
            below = work[rest:, :]
            lanes = lax.broadcasted_iota(jnp.int32, below.shape, 1)
            below = jnp.where((lanes >= start) & (lanes < end), 0.0, below)
            work[rest:, :] = below - change[rest:, :]


def load_matrix(a_ref, out_ref):
    @pl.loop(0, out_ref.shape[0] // BLOCK)
    def _(i):
        at = pl.ds(pl.multiple_of(i * BLOCK, BLOCK), BLOCK)
        out_ref[at, :] = a_ref[at, :]


def load_covariance(down_ref, across_ref, out_ref):
    size = out_ref.shape[0]
    chunk = 4 * BLOCK if size % (4 * BLOCK) == 0 else BLOCK

    @pl.loop(0, size // BLOCK)
    def _(i):
        first = pl.multiple_of(i * BLOCK, BLOCK)
        at = pl.ds(first, BLOCK)
        for start in range(0, size, chunk):

            @pl.when(start + chunk > first)
            def _():
                delta_x = down_ref[at, 0:1] - across_ref[0:1, start : start + chunk]
                delta_y = down_ref[at, 1:2] - across_ref[1:2, start : start + chunk]
                value = jnp.exp(-jnp.sqrt(delta_x * delta_x + delta_y * delta_y) * (1.0 / range_length))
                row = lax.broadcasted_iota(jnp.int32, value.shape, 0) + first
                col = lax.broadcasted_iota(jnp.int32, value.shape, 1) + start
                out_ref[at, start : start + chunk] = value + jnp.where(row == col, nugget, 0.0)


def factor_kernel(load, *refs):
    *sources, out_ref, work, left, right = refs
    size = out_ref.shape[0]
    blocks = size // BLOCK
    chunk = 4 * BLOCK if size % (4 * BLOCK) == 0 else BLOCK
    load(*sources, out_ref)

    @pl.loop(0, blocks)
    def _(k):
        start = pl.multiple_of(k * BLOCK, BLOCK)
        at = pl.ds(start, BLOCK)
        work[...] = out_ref[at, at]
        leaf(work)
        row = lax.broadcasted_iota(jnp.int32, (BLOCK, BLOCK), 0)
        col = lax.broadcasted_iota(jnp.int32, (BLOCK, BLOCK), 1)
        inverse = jnp.where(row >= col, work[...], 0.0)
        high, low = split(inverse)
        both = jnp.concatenate([high, high, low], axis=1)
        p_high, p_low = split(out_ref[at, :])
        stacked = jnp.concatenate([p_high, p_low, p_high], axis=0)
        panel = jnp.dot(both, stacked, preferred_element_type=jnp.float32)
        wide = lax.broadcasted_iota(jnp.int32, (BLOCK, size), 1)
        out_ref[at, :] = jnp.where(wide < start, panel, 0.0)
        out_ref[at, at] = inverse
        r_high, r_low = split(panel)
        left[0:BLOCK, :] = r_high
        left[BLOCK : 2 * BLOCK, :] = r_high
        left[2 * BLOCK :, :] = r_low
        right[0:BLOCK, :] = r_high
        right[BLOCK : 2 * BLOCK, :] = r_low
        right[2 * BLOCK :, :] = r_high
        right[0:BLOCK, at] = high
        right[BLOCK : 2 * BLOCK, at] = low
        right[2 * BLOCK :, at] = high

        def update(first, count):
            rows = pl.ds(pl.multiple_of(first * BLOCK, BLOCK), count * BLOCK)
            out_ref[rows, at] = jnp.zeros((count * BLOCK, BLOCK), jnp.float32)
            for begin in range(0, size, chunk):

                @pl.when((begin <= start) | (begin + chunk > first * BLOCK))
                def _():
                    span = slice(begin, begin + chunk)
                    out_ref[rows, span] = out_ref[rows, span] - contract_rows(left[:, rows], right[:, span])

        rest = blocks - 1 - k

        @pl.loop(0, rest // 2)
        def _(pair):
            update(k + 1 + 2 * pair, 2)

        @pl.when(rest % 2 == 1)
        def _():
            update(blocks - 1, 1)


def inverse_factor(load, size, *sources):
    return pl.pallas_call(
        functools.partial(factor_kernel, load),
        out_shape=jax.ShapeDtypeStruct((size, size), jnp.float32),
        in_specs=[pl.BlockSpec(memory_space=pltpu.VMEM)] * len(sources),
        out_specs=pl.BlockSpec(memory_space=pltpu.VMEM),
        scratch_shapes=[
            pltpu.VMEM((BLOCK, BLOCK), jnp.float32),
            pltpu.VMEM((3 * BLOCK, size), jnp.bfloat16),
            pltpu.VMEM((3 * BLOCK, size), jnp.bfloat16),
        ],
        compiler_params=pltpu.CompilerParams(vmem_limit_bytes=48 * 1024 * 1024),
        cost_estimate=pl.CostEstimate(
            flops=size * 400000 + 6 * size**3, bytes_accessed=8 * size * size, transcendentals=0
        ),
    )(*sources)


def high_dot(spec, first, second):
    return jnp.einsum(spec, first, second, precision=lax.Precision.HIGH, preferred_element_type=jnp.float32)


def spread(value, n_row, n_col, row_tiles, row_index, col_index):
    root = col_index // row_tiles
    reached = n_row
    step = n_row // 2
    while step >= 1:
        pairs = []
        for b in range(n_col):
            source = b // row_tiles
            for a in range(n_row):
                if (a ^ source) % reached == 0:
                    pairs.append((a * n_col + b, (a ^ step) * n_col + b))
        moved = lax.ppermute(value, ("row", "col"), pairs)
        gets = ((row_index ^ root) % reached) == step
        value = jnp.where(gets, moved, value)
        reached = step
        step //= 2
    return value


def shards(diag_coords, panel_coords, test_matrix, ranks):
    points = diag_coords.shape[1]
    row_tiles = panel_coords.shape[1]
    width = test_matrix.shape[2]
    share = test_matrix.shape[1]
    n_row = lax.axis_size("row")
    n_col = lax.axis_size("col")
    assert row_tiles in (1, 2) and n_col == n_row * row_tiles and n_col % 4 == 0
    row_index = lax.axis_index("row")
    col_index = lax.axis_index("col")
    own = (col_index ^ (col_index // 2) ^ row_index) % row_tiles
    tile = row_index * row_tiles + own

    halves = jnp.stack(
        [panel_coords[0] // 256, panel_coords[0] % 256, panel_coords[1] // 256, panel_coords[1] % 256], axis=-1
    ).astype(jnp.bfloat16)
    halves = jnp.pad(halves, ((0, 0), (0, 0), (0, 128 - 4)))
    gathered = lax.all_gather(jnp.concatenate([test_matrix, halves], axis=2), "col", axis=1, tiled=True)
    across = diag_coords.astype(jnp.float32)
    lower_inverse = inverse_factor(load_covariance, points, across.T, across)

    columns = jnp.arange(width, dtype=jnp.int32)
    rank = lax.dynamic_index_in_dim(ranks, tile, 0, keepdims=False)
    mask = (columns < rank).astype(jnp.float32)
    mine = lax.dynamic_index_in_dim(gathered, own, 0, keepdims=False)
    tests = mine[:, :width] * mask.astype(jnp.bfloat16)[None, :]
    halves = mine[:, width : width + 4].astype(jnp.float32)
    tile_x = halves[:, 0:1] * 256.0 + halves[:, 1:2]
    tile_y = halves[:, 2:3] * 256.0 + halves[:, 3:4]
    delta_x = tile_x - across[0][None, :]
    delta_y = tile_y - across[1][None, :]
    block = jnp.exp(-jnp.sqrt(delta_x * delta_x + delta_y * delta_y) / range_length)

    weights = high_dot("mk,mr->kr", lower_inverse, tests.astype(jnp.float32))
    sample = high_dot("nk,kr->nr", block, weights)
    gram = high_dot("nr,ns->rs", sample, sample)
    shift = shift_ratio * jnp.sum(sample * sample) / rank.astype(jnp.float32)
    shifted = gram + jnp.diag(shift * mask + 1.0 - mask)
    factor_inverse = inverse_factor(load_matrix, width, shifted)
    basis = high_dot("nr,sr->ns", sample, factor_inverse).astype(jnp.bfloat16)
    pieces = basis.reshape(n_col, share, width)

    def swap(value, distance):
        return lax.ppermute(value, "col", [(b, b ^ distance) for b in range(n_col)])

    lefts = [lax.dynamic_index_in_dim(pieces, col_index, 0, keepdims=False)]
    if row_tiles > 1:
        lefts.append(swap(lax.dynamic_index_in_dim(pieces, col_index ^ 1, 0, keepdims=False), 1))
    col_left = spread(basis, n_row, n_col, row_tiles, row_index, col_index)

    projected = high_dot("nm,nr->mr", block, basis.astype(jnp.float32))
    half = points // 2
    upper = high_dot("km,mr->kr", lower_inverse[:half, :half], projected[:half]).astype(jnp.bfloat16)
    lower = high_dot("km,mr->kr", lower_inverse[half:], projected).astype(jnp.bfloat16)
    coeff = jnp.concatenate([upper, lower])
    coeffs = [coeff]
    if row_tiles > 1:
        coeffs.append(jnp.concatenate([swap(upper, 1), swap(lower, 2)]))
    col_coeff = spread(coeff, n_row, n_col, row_tiles, row_index, col_index)

    def ordered(entries):
        stack = jnp.stack(entries)
        return jnp.roll(stack, own, axis=0) if row_tiles > 1 else stack

    left = ordered(lefts)
    row_coeff = ordered(coeffs)
    core = jnp.einsum("inr,ns->irs", row_coeff, col_coeff, preferred_element_type=jnp.float32)
    core = core.astype(jnp.bfloat16)
    many_left = jnp.broadcast_to(col_left[None], (row_tiles,) + col_left.shape)
    update = jnp.einsum("ins,irs->inr", many_left, core, preferred_element_type=jnp.float32)
    return (left, update.astype(jnp.bfloat16)[:, None])


def solution(mesh):
    in_specs = (P(), P(None, "row", "col"), P("row", "col", None), P())
    out_specs = (P("row", "col", None), P("row", "col", None, None))
    return jax.shard_map(shards, mesh=mesh, in_specs=in_specs, out_specs=out_specs, check_vma=False)
```

```python
import functools

import jax
import jax.numpy as jnp
from jax import lax
from jax.experimental import pallas as pl
from jax.experimental.pallas import tpu as pltpu
from jax.sharding import PartitionSpec as P

range_length = 409.6
nugget = 0.5
shift_ratio = 0.01
BLOCK = 128
SUB = 8


def split(value):
    high = value.astype(jnp.bfloat16)
    low = (value - high.astype(jnp.float32)).astype(jnp.bfloat16)
    return high, low


def contract_rows(first, second):
    return lax.dot_general(first, second, (((0,), (0,)), ((), ())), preferred_element_type=jnp.float32)


def leaf(work):
    lane = lax.broadcasted_iota(jnp.int32, (SUB, BLOCK), 1)
    sub = lax.broadcasted_iota(jnp.int32, (SUB, BLOCK), 0)
    for panel in range(BLOCK // SUB):
        start = panel * SUB
        end = start + SUB
        spots = [at for at in (start, end, end + SUB) if at < BLOCK]
        loaded = [work[at : at + SUB, :] for at in spots]
        inside = (lane >= start) & (lane < end)
        columns = [
            [jnp.broadcast_to(part[:, start + j : start + j + 1], (SUB, BLOCK)) for j in range(SUB)]
            for part in loaded
        ]
        own = (lane - start == sub).astype(jnp.float32)
        rows = [jnp.where(inside, own if g == 0 else 0.0, part) for g, part in enumerate(loaded)]
        pivots = jnp.ones((SUB, BLOCK), jnp.float32)
        for k in range(SUB):
            pivot = jnp.broadcast_to(columns[0][k][k : k + 1, :], (SUB, BLOCK))
            pivots = jnp.where(sub == k, pivot, pivots)
            ratio = pl.reciprocal(pivot, approx=True)
            ratio = ratio * (2.0 - pivot * ratio)
            factors = [part[k] * ratio for part in columns]
            factors[0] = jnp.where(sub > k, factors[0], 0.0)
            top = rows[0][k : k + 1, :]
            rows = [part - factor * top for part, factor in zip(rows, factors)]
            for j in range(k + 1, SUB):
                entry = columns[0][j][k : k + 1, :]
                for part, factor in zip(columns, factors):
                    part[j] = part[j] - factor * entry
        scaled = rows[0] * lax.rsqrt(pivots)
        work[start:end, :] = scaled
        for at, part in zip(spots[1:], rows[1:]):
            work[at : at + SUB, :] = part
        rest = end + 2 * SUB
        if rest < BLOCK:
            right = jnp.where(lane >= rest, scaled, 0.0)
            change = lax.dot_general(
                right, scaled, (((0,), (0,)), ((), ())),
                precision=lax.Precision.HIGHEST, preferred_element_type=jnp.float32,
            )
            below = work[rest:, :]
            lanes = lax.broadcasted_iota(jnp.int32, below.shape, 1)
            below = jnp.where((lanes >= start) & (lanes < end), 0.0, below)
            work[rest:, :] = below - change[rest:, :]


def load_matrix(a_ref, out_ref):
    @pl.loop(0, out_ref.shape[0] // BLOCK)
    def _(i):
        at = pl.ds(pl.multiple_of(i * BLOCK, BLOCK), BLOCK)
        out_ref[at, :] = a_ref[at, :]


def load_covariance(down_ref, across_ref, out_ref):
    size = out_ref.shape[0]
    chunk = 4 * BLOCK if size % (4 * BLOCK) == 0 else BLOCK

    @pl.loop(0, size // BLOCK)
    def _(i):
        first = pl.multiple_of(i * BLOCK, BLOCK)
        at = pl.ds(first, BLOCK)
        for start in range(0, size, chunk):

            @pl.when(start + chunk > first)
            def _():
                delta_x = down_ref[at, 0:1] - across_ref[0:1, start : start + chunk]
                delta_y = down_ref[at, 1:2] - across_ref[1:2, start : start + chunk]
                value = jnp.exp(-jnp.sqrt(delta_x * delta_x + delta_y * delta_y) * (1.0 / range_length))
                row = lax.broadcasted_iota(jnp.int32, value.shape, 0) + first
                col = lax.broadcasted_iota(jnp.int32, value.shape, 1) + start
                out_ref[at, start : start + chunk] = value + jnp.where(row == col, nugget, 0.0)


def factor_kernel(load, *refs):
    *sources, out_ref, work, left, right = refs
    size = out_ref.shape[0]
    blocks = size // BLOCK
    load(*sources, out_ref)

    @pl.loop(0, blocks)
    def _(k):
        start = pl.multiple_of(k * BLOCK, BLOCK)
        at = pl.ds(start, BLOCK)
        work[...] = out_ref[at, at]
        leaf(work)
        row = lax.broadcasted_iota(jnp.int32, (BLOCK, BLOCK), 0)
        col = lax.broadcasted_iota(jnp.int32, (BLOCK, BLOCK), 1)
        inverse = jnp.where(row >= col, work[...], 0.0)
        high, low = split(inverse)
        both = jnp.concatenate([high, high, low], axis=1)
        p_high, p_low = split(out_ref[at, :])
        stacked = jnp.concatenate([p_high, p_low, p_high], axis=0)
        panel = jnp.dot(both, stacked, preferred_element_type=jnp.float32)
        wide = lax.broadcasted_iota(jnp.int32, (BLOCK, size), 1)
        out_ref[at, :] = jnp.where(wide < start, panel, 0.0)
        out_ref[at, at] = inverse
        r_high, r_low = split(panel)
        left[0:BLOCK, :] = r_high
        left[BLOCK : 2 * BLOCK, :] = r_high
        left[2 * BLOCK :, :] = r_low
        right[0:BLOCK, :] = r_high
        right[BLOCK : 2 * BLOCK, :] = r_low
        right[2 * BLOCK :, :] = r_high
        right[0:BLOCK, at] = high
        right[BLOCK : 2 * BLOCK, at] = low
        right[2 * BLOCK :, at] = high

        def update(first, count):
            rows = pl.ds(pl.multiple_of(first * BLOCK, BLOCK), count * BLOCK)
            out_ref[rows, at] = jnp.zeros((count * BLOCK, BLOCK), jnp.float32)
            out_ref[rows, :] = out_ref[rows, :] - contract_rows(left[:, rows], right[...])

        rest = blocks - 1 - k

        @pl.loop(0, rest // 4)
        def _(four):
            update(k + 1 + 4 * four, 4)

        @pl.when(rest % 4 >= 2)
        def _():
            update(k + 1 + rest // 4 * 4, 2)

        @pl.when(rest % 2 == 1)
        def _():
            update(blocks - 1, 1)


def inverse_factor(load, size, *sources):
    return pl.pallas_call(
        functools.partial(factor_kernel, load),
        out_shape=jax.ShapeDtypeStruct((size, size), jnp.float32),
        in_specs=[pl.BlockSpec(memory_space=pltpu.VMEM)] * len(sources),
        out_specs=pl.BlockSpec(memory_space=pltpu.VMEM),
        scratch_shapes=[
            pltpu.VMEM((BLOCK, BLOCK), jnp.float32),
            pltpu.VMEM((3 * BLOCK, size), jnp.bfloat16),
            pltpu.VMEM((3 * BLOCK, size), jnp.bfloat16),
        ],
        compiler_params=pltpu.CompilerParams(vmem_limit_bytes=48 * 1024 * 1024),
        cost_estimate=pl.CostEstimate(
            flops=size * 400000 + 6 * size**3, bytes_accessed=8 * size * size, transcendentals=0
        ),
    )(*sources)


def high_dot(spec, first, second):
    return jnp.einsum(spec, first, second, precision=lax.Precision.HIGH, preferred_element_type=jnp.float32)


def spread(value, n_row, n_col, row_tiles, row_index, col_index):
    root = col_index // row_tiles
    reached = n_row
    step = n_row // 2
    while step >= 1:
        pairs = []
        for b in range(n_col):
            source = b // row_tiles
            for a in range(n_row):
                if (a ^ source) % reached == 0:
                    pairs.append((a * n_col + b, (a ^ step) * n_col + b))
        moved = lax.ppermute(value, ("row", "col"), pairs)
        gets = ((row_index ^ root) % reached) == step
        value = jnp.where(gets, moved, value)
        reached = step
        step //= 2
    return value


def shards(diag_coords, panel_coords, test_matrix, ranks):
    points = diag_coords.shape[1]
    row_tiles = panel_coords.shape[1]
    width = test_matrix.shape[2]
    share = test_matrix.shape[1]
    n_row = lax.axis_size("row")
    n_col = lax.axis_size("col")
    assert row_tiles in (1, 2) and n_col == n_row * row_tiles and n_col % 4 == 0
    row_index = lax.axis_index("row")
    col_index = lax.axis_index("col")
    own = (col_index ^ (col_index // 2) ^ row_index) % row_tiles
    tile = row_index * row_tiles + own

    halves = jnp.stack(
        [panel_coords[0] // 256, panel_coords[0] % 256, panel_coords[1] // 256, panel_coords[1] % 256], axis=-1
    ).astype(jnp.bfloat16)
    halves = jnp.pad(halves, ((0, 0), (0, 0), (0, 128 - 4)))
    gathered = lax.all_gather(jnp.concatenate([test_matrix, halves], axis=2), "col", axis=1, tiled=True)
    across = diag_coords.astype(jnp.float32)
    lower_inverse = inverse_factor(load_covariance, points, across.T, across)

    columns = jnp.arange(width, dtype=jnp.int32)
    rank = lax.dynamic_index_in_dim(ranks, tile, 0, keepdims=False)
    mask = (columns < rank).astype(jnp.float32)
    mine = lax.dynamic_index_in_dim(gathered, own, 0, keepdims=False)
    tests = mine[:, :width] * mask.astype(jnp.bfloat16)[None, :]
    halves = mine[:, width : width + 4].astype(jnp.float32)
    tile_x = halves[:, 0:1] * 256.0 + halves[:, 1:2]
    tile_y = halves[:, 2:3] * 256.0 + halves[:, 3:4]
    delta_x = tile_x - across[0][None, :]
    delta_y = tile_y - across[1][None, :]
    block = jnp.exp(-jnp.sqrt(delta_x * delta_x + delta_y * delta_y) / range_length)

    weights = high_dot("mk,mr->kr", lower_inverse, tests.astype(jnp.float32))
    sample = high_dot("nk,kr->nr", block, weights)
    gram = high_dot("nr,ns->rs", sample, sample)
    shift = shift_ratio * jnp.sum(sample * sample) / rank.astype(jnp.float32)
    shifted = gram + jnp.diag(shift * mask + 1.0 - mask)
    factor_inverse = inverse_factor(load_matrix, width, shifted)
    basis = high_dot("nr,sr->ns", sample, factor_inverse).astype(jnp.bfloat16)
    pieces = basis.reshape(n_col, share, width)

    def swap(value, distance):
        return lax.ppermute(value, "col", [(b, b ^ distance) for b in range(n_col)])

    lefts = [lax.dynamic_index_in_dim(pieces, col_index, 0, keepdims=False)]
    if row_tiles > 1:
        lefts.append(swap(lax.dynamic_index_in_dim(pieces, col_index ^ 1, 0, keepdims=False), 1))
    col_left = spread(basis, n_row, n_col, row_tiles, row_index, col_index)

    projected = high_dot("nm,nr->mr", block, basis.astype(jnp.float32))
    half = points // 2
    upper = high_dot("km,mr->kr", lower_inverse[:half, :half], projected[:half]).astype(jnp.bfloat16)
    lower = high_dot("km,mr->kr", lower_inverse[half:], projected).astype(jnp.bfloat16)
    coeff = jnp.concatenate([upper, lower])
    coeffs = [coeff]
    if row_tiles > 1:
        coeffs.append(jnp.concatenate([swap(upper, 1), swap(lower, 2)]))
    col_coeff = spread(coeff, n_row, n_col, row_tiles, row_index, col_index)

    def ordered(entries):
        stack = jnp.stack(entries)
        return jnp.roll(stack, own, axis=0) if row_tiles > 1 else stack

    left = ordered(lefts)
    row_coeff = ordered(coeffs)
    core = jnp.einsum("inr,ns->irs", row_coeff, col_coeff, preferred_element_type=jnp.float32)
    core = core.astype(jnp.bfloat16)
    many_left = jnp.broadcast_to(col_left[None], (row_tiles,) + col_left.shape)
    update = jnp.einsum("ins,irs->inr", many_left, core, preferred_element_type=jnp.float32)
    return (left, update.astype(jnp.bfloat16)[:, None])


def solution(mesh):
    in_specs = (P(), P(None, "row", "col"), P("row", "col", None), P())
    out_specs = (P("row", "col", None), P("row", "col", None, None))
    return jax.shard_map(shards, mesh=mesh, in_specs=in_specs, out_specs=out_specs, check_vma=False)
```
